32 devices in a mesh: heads: 2 (over y), seq: 16 (over z, x, core).
Axes of the slice: x: 2, y: 2, z: 4, core: 2. Of those that a mesh axis runs over, the one named last changes fastest.
Arguments:
- queries: bfloat16 [2, 6144, 4096], P(None, 'seq', 'heads'), may hold values from -72 to 72, as said below
- key_rows: bfloat16 [2, 6144, 4096], P(None, 'seq', 'heads'), may hold values from -6.06 to 6.06, as said below
- value_rows: bfloat16 [2, 6144, 4096], P(None, 'seq', 'heads'), may hold values from -6 to 6
- step_rates: float32 [8, 2, 6144], P('heads', None, 'seq'), may hold values from 0.0001 to 0.001
- w_gate: float32 [8, 512, 512], P('heads', 'seq'), may hold values from -0.25 to 0.25
- w_up: float32 [8, 512, 512], P('heads', 'seq'), may hold values from -0.25 to 0.25
- w_down: float32 [8, 512, 512], P('heads', 'seq'), may hold values from -0.25 to 0.25
- out_gain: float32 [4096], P('heads'), may hold values from 0.5 to 1.5
Outputs:
- layer_out: bfloat16 [2, 6144, 4096], P(None, 'seq', 'heads')
- new_gate: float32 [8, 512, 512], P('heads', 'seq')
- new_up: float32 [8, 512, 512], P('heads', 'seq')
- new_down: float32 [8, 512, 512], P('heads', 'seq')
The draws below stay inside these ranges and needn't reach their ends.
Inputs may be any that keep to these rules, and one draw needn't show every extreme that they name: `queries`: entries of order one with a few larger ones. `key_rows`: entries of order one.
All inputs are finite; a program needn't handle non-finite values.
Results may differ from the reference program's by a relative error of at most 0.0069.
The reference program's roundings to bfloat16 on the way count: a program that leaves them out, or rounds other values in their place, can miss the bound.
Values may be sent and summed in bfloat16 or wider, within the bound.
A program may use at most 192 MiB of HBM per device.

```python
import math
import jax
import jax.numpy as jnp
from jax import lax

HEADS = 8
DH = 512
HID = 512
WINDOW = 768
STRETCHES = 2
TOK_DEV = 384
CTOK = 6144


def paired_draw(key):
    query_key = jax.random.fold_in(key, 11)
    keys_key = jax.random.fold_in(key, 23)
    full_shape = (STRETCHES, CTOK, HEADS * DH)
    keys_base = jnp.clip(jax.random.normal(keys_key, full_shape, jnp.float32), -6.0, 6.0)
    queries_base = jnp.clip(jax.random.normal(query_key, full_shape, jnp.float32), -6.0, 6.0)
    return (queries_base, keys_base)


def draw_queries(key, part):
    return paired_draw(key)[0].astype(jnp.bfloat16)


def draw_key_rows(key, part):
    return paired_draw(key)[1].astype(jnp.bfloat16)


def block_levels(own_key, dims, cuts, least, largest):
    loudness = 1.0
    for dim, shards_of in cuts:
        steps = jax.random.uniform(jax.random.fold_in(jax.random.fold_in(own_key, 6), dim), (shards_of,), jnp.float32, least / len(cuts), largest / len(cuts))
        loudness = loudness * jnp.repeat(jnp.exp(steps), dims[dim] // shards_of).reshape((-1,) + (1,) * (len(dims) - 1 - dim))
    return loudness


def gaussian(own_key, dims, spread, reach, cuts=(), held_as=jnp.bfloat16):
    drawn = jax.random.normal(own_key, dims, jnp.float32) * spread
    if len(cuts) > 0:
        drawn = block_levels(own_key, dims, cuts, -0.22, 0.18) * drawn
    return jnp.clip(drawn, min=-reach, max=reach).astype(held_as)


def setup_inputs(seed: int = 0) -> dict:
    streams_of = jax.random.split(jax.random.key(seed), 9)
    return {
        "queries": draw_queries(jax.random.fold_in(streams_of[8], 71), 0),
        "key_rows": draw_key_rows(jax.random.fold_in(streams_of[8], 71), 0),
        "value_rows": gaussian(streams_of[2], (STRETCHES, CTOK, HEADS * DH), 1.0, 6.0, ((1, 16), (2, 2))),
        "step_rates": jnp.clip(jnp.exp(math.log(0.001) - 2.3025852 * jax.random.uniform(streams_of[3], (HEADS, STRETCHES, CTOK), jnp.float32) ** block_levels(streams_of[3], (HEADS, STRETCHES, CTOK), ((0, 2), (2, 16)), -0.2, 0.2)), 0.0001, 0.001),
        "w_gate": gaussian(streams_of[4], (HEADS, DH, HID), DH ** -0.5, 0.25, ((0, 2), (1, 16)), jnp.float32),
        "w_up": gaussian(streams_of[5], (HEADS, DH, HID), DH ** -0.5, 0.25, ((0, 2), (1, 16)), jnp.float32),
        "w_down": gaussian(streams_of[6], (HEADS, HID, DH), HID ** -0.5, 0.25, ((0, 2), (1, 16)), jnp.float32),
        "out_gain": jnp.clip(1.0 + 0.1 * jax.random.normal(streams_of[7], (HEADS * DH,), jnp.float32), 0.5, 1.5),
    }


NORM_EPS = 1e-05
MASKED = -1e+30

def apply_head(inputs, copies):
    gate_copy, up_copy, down_copy = copies
    gate_pre = jnp.dot(inputs, gate_copy, preferred_element_type=jnp.float32)
    up_pre = jnp.dot(inputs, up_copy, preferred_element_type=jnp.float32)
    active = (jax.nn.silu(gate_pre) * up_pre).astype(jnp.bfloat16)
    return jnp.dot(active, down_copy, preferred_element_type=jnp.float32)

def grads_head(key_in, value_in, rate_in, copies):
    gate_copy, up_copy, down_copy = copies
    gate_pre = jnp.dot(key_in, gate_copy, preferred_element_type=jnp.float32)
    up_pre = jnp.dot(key_in, up_copy, preferred_element_type=jnp.float32)
    sigmoid_g = jax.nn.sigmoid(gate_pre)
    silu_g = gate_pre * sigmoid_g
    active = (silu_g * up_pre).astype(jnp.bfloat16)
    target = (-(rate_in[:, None] * value_in.astype(jnp.float32))).astype(jnp.bfloat16)
    grad_down = jnp.dot(active.T, target, preferred_element_type=jnp.float32)
    back = jnp.dot(target, down_copy.T, preferred_element_type=jnp.float32)
    d_gate = (back * up_pre * sigmoid_g * (1.0 + gate_pre * (1.0 - sigmoid_g))).astype(jnp.bfloat16)
    d_up = (back * silu_g).astype(jnp.bfloat16)
    grad_gate = jnp.dot(key_in.T, d_gate, preferred_element_type=jnp.float32)
    grad_up = jnp.dot(key_in.T, d_up, preferred_element_type=jnp.float32)
    return (grad_gate, grad_up, grad_down)

def head_pass(packed):
    query_head, key_head, value_head, rate_head, gate_master, up_master, down_master = packed
    masters = (gate_master, up_master, down_master)
    copies = tuple((member.astype(jnp.bfloat16) for member in masters))
    first_out = apply_head(query_head[0], copies)
    gradients = grads_head(key_head[0], value_head[0], rate_head[0], copies)
    updated = tuple((master - gradient for master, gradient in zip(masters, gradients)))
    second_out = apply_head(query_head[1], tuple((member.astype(jnp.bfloat16) for member in updated)))
    return (jnp.stack([first_out, second_out]), updated[0], updated[1], updated[2])

def window_reference(queries, key_rows, value_rows):
    total_rows = STRETCHES * CTOK
    query_flat = queries.reshape(total_rows, HEADS, DH)
    zero_rows = jnp.zeros((WINDOW, HEADS, DH), jnp.bfloat16)
    key_padded = jnp.concatenate([zero_rows, key_rows.reshape(total_rows, HEADS, DH)], axis=0)
    value_padded = jnp.concatenate([zero_rows, value_rows.reshape(total_rows, HEADS, DH)], axis=0)

    def query_block(block_index):
        row_start = (block_index * TOK_DEV).astype(jnp.int32)
        query_part = lax.dynamic_slice_in_dim(query_flat, row_start, TOK_DEV, 0)
        key_part = lax.dynamic_slice_in_dim(key_padded, row_start, TOK_DEV + WINDOW, 0)
        value_part = lax.dynamic_slice_in_dim(value_padded, row_start, TOK_DEV + WINDOW, 0)
        scores = jnp.einsum('qhd,khd->hqk', query_part.astype(jnp.float32), key_part.astype(jnp.float32)) * DH ** (-0.5)
        query_pos = jnp.arange(TOK_DEV, dtype=jnp.int32)[:, None]
        key_pos = jnp.arange(TOK_DEV + WINDOW, dtype=jnp.int32)[None, :]
        allowed = (key_pos > query_pos) & (key_pos <= query_pos + WINDOW) & (row_start + key_pos - WINDOW >= 0)
        scores = jnp.where(allowed[None], scores, MASKED)
        row_peak = lax.optimization_barrier(jnp.max(scores, axis=-1, keepdims=True))
        weights = jnp.exp(scores - row_peak)
        soft_weights = (weights / lax.optimization_barrier(jnp.sum(weights, axis=-1, keepdims=True))).astype(jnp.bfloat16)
        return jnp.einsum('hqk,khd->qhd', soft_weights.astype(jnp.float32), value_part.astype(jnp.float32))
    blocks_out = lax.map(query_block, jnp.arange(total_rows // TOK_DEV, dtype=jnp.int32))
    return blocks_out.reshape(STRETCHES, CTOK, HEADS * DH)

def reference(queries, key_rows, value_rows, step_rates, w_gate, w_up, w_down, out_gain):

    def by_head(array):
        return array.reshape(STRETCHES, CTOK, HEADS, DH).transpose(2, 0, 1, 3)
    fast_out, new_gate, new_up, new_down = lax.map(head_pass, (by_head(queries), by_head(key_rows), by_head(value_rows), step_rates, w_gate, w_up, w_down))
    fast_out = fast_out.transpose(1, 2, 0, 3).reshape(STRETCHES, CTOK, HEADS * DH)
    row_power = lax.optimization_barrier(jnp.sum(fast_out * fast_out, axis=-1, keepdims=True))
    normed = fast_out * out_gain * lax.rsqrt(row_power / (HEADS * DH) + NORM_EPS)
    attended = window_reference(queries, key_rows, value_rows)
    layer_out = (normed + attended).astype(jnp.bfloat16)
    return (layer_out, new_gate, new_up, new_down)
```

```python
import functools

import jax
import jax.numpy as jnp
from jax import lax
from jax.experimental import pallas as pl
from jax.experimental.pallas import tpu as pltpu
from jax.sharding import PartitionSpec as P

WINDOW = 768
NORM_EPS = 1e-05
MASKED = -1e30
VMEM = 56 * 1024 * 1024
F32 = jnp.float32
BF16 = jnp.bfloat16


def dot(a, b, contract=((1,), (0,))):
    return lax.dot_general(a, b, (contract, ((), ())), preferred_element_type=F32)


def passed_along(value, axis, steps):
    count = lax.axis_size(axis)
    pairs = [(source, (source + steps) % count) for source in range(count)]
    return lax.ppermute(value, axis, pairs)


def groups():
    count = lax.axis_size("seq")
    near = 2 if count % 2 == 0 else 1
    far = count // near
    inside = [[i * near + j for j in range(near)] for i in range(far)]
    across = [[i * near + j for i in range(far)] for j in range(near)]
    return inside, across


def gather_two_level(value):
    inside, across = groups()
    return lax.all_gather(value, "seq", axis=0)[None]


def scatter_two_level(value):
    inside, across = groups()
    return lax.psum_scatter(value[0], "seq", scatter_dimension=0)


def params():
    return pltpu.CompilerParams(vmem_limit_bytes=VMEM)


def weights_of(w_ref, which):
    near, far = w_ref.shape[:2]
    return jnp.concatenate(
        [w_ref[i % near, i // near, 0, which] for i in range(near * far)], axis=0
    )


def grads_kernel(w_ref, k_ref, v_ref, r_ref, out_ref):
    head = pl.program_id(0)
    near, far, _, _, rows, cols = w_ref.shape
    k = k_ref[0]
    lane = lax.broadcasted_iota(jnp.int32, r_ref.shape, 1)
    rate = jnp.sum(jnp.where(lane == head, r_ref[...], 0.0), axis=1, keepdims=True)
    g = dot(k, weights_of(w_ref, 0))
    u = dot(k, weights_of(w_ref, 1))
    target = (-(rate * v_ref[0].astype(F32))).astype(BF16)
    back = dot(target, weights_of(w_ref, 2), ((1,), (1,)))
    sig = jax.nn.sigmoid(g)
    silu = g * sig
    active = (silu * u).astype(BF16)
    d_gate = (back * u * sig * (1.0 + g * (1.0 - sig))).astype(BF16)
    d_up = (back * silu).astype(BF16)
    first = ((0,), (0,))
    pairs = ((active, target), (k, d_gate), (k, d_up))
    for which, (left, right) in zip((2, 0, 1), pairs):
        full = dot(left, right, first).astype(BF16)
        for i in range(near * far):
            out_ref[i % near, i // near, 0, which] = full[i * rows : (i + 1) * rows]


def fast_grads(copies, key_rows, value_rows, rates):
    near, far, heads, _, rows, cols = copies.shape
    tok = key_rows.shape[1]
    size = near * far * rows
    w_spec = pl.BlockSpec((near, far, 1, 3, rows, cols), lambda h: (0, 0, h, 0, 0, 0))
    t_spec = pl.BlockSpec((1, tok, size), lambda h: (0, 0, h))
    return pl.pallas_call(
        grads_kernel,
        grid=(heads,),
        in_specs=[w_spec, t_spec, t_spec, pl.BlockSpec(rates.shape, lambda h: (0, 0))],
        out_specs=w_spec,
        out_shape=jax.ShapeDtypeStruct(copies.shape, BF16),
        compiler_params=params(),
        cost_estimate=pl.CostEstimate(
            flops=heads * tok * size * cols * 12,
            bytes_accessed=copies.size * 4 + tok * heads * size * 4,
            transcendentals=heads * tok * cols,
        ),
        name="fast_grads",
    )(copies, key_rows, value_rows, rates)


def apply_kernel(w_ref, q_ref, out_ref, power_ref):
    head = pl.program_id(0)
    q = q_ref[0]
    g = dot(q, weights_of(w_ref, 0))
    u = dot(q, weights_of(w_ref, 1))
    active = (g * jax.nn.sigmoid(g) * u).astype(BF16)
    out = dot(active, weights_of(w_ref, 2))
    out_ref[...] = out
    power = jnp.sum(out * out, axis=1, keepdims=True)

    @pl.when(head == 0)
    def _():
        power_ref[...] = power

    @pl.when(head > 0)
    def _():
        power_ref[...] += power


def fast_apply(copies, queries, stretch):
    near, far, heads, _, rows, cols = copies.shape
    tok = queries.shape[1]
    size = near * far * rows
    return pl.pallas_call(
        apply_kernel,
        grid=(heads,),
        in_specs=[
            pl.BlockSpec((near, far, 1, 3, rows, cols), lambda h: (0, 0, h, 0, 0, 0)),
            pl.BlockSpec((1, tok, size), lambda h: (stretch, 0, h)),
        ],
        out_specs=[
            pl.BlockSpec((tok, size), lambda h: (0, h)),
            pl.BlockSpec((tok, 1), lambda h: (0, 0)),
        ],
        out_shape=[
            jax.ShapeDtypeStruct((tok, heads * size), F32),
            jax.ShapeDtypeStruct((tok, 1), F32),
        ],
        compiler_params=params(),
        cost_estimate=pl.CostEstimate(
            flops=heads * tok * size * cols * 6,
            bytes_accessed=copies.size * 2 + tok * heads * size * 6,
            transcendentals=heads * tok * cols,
        ),
        name="fast_apply",
    )(copies, queries)


def attend_kernel(hops, stretch, seq_ref, q_ref, *refs):
    keys = refs[: hops + 1]
    values = refs[hops + 1 : 2 * hops + 2]
    out_ref = refs[-1]
    q = q_ref[0]
    tok, size = q.shape
    row = lax.broadcasted_iota(jnp.int32, (tok, tok), 0)
    col = lax.broadcasted_iota(jnp.int32, (tok, tok), 1)
    scores = []
    for hop in range(hops + 1):
        s = dot(q, keys[hop][0], ((1,), (1,))) * size ** (-0.5)
        place = col - hop * tok
        if hop == 0:
            s = jnp.where(place <= row, s, MASKED)
        if (hop + 1) * tok > WINDOW:
            s = jnp.where(place > row - WINDOW, s, MASKED)
        if hop > 0 and stretch == 0:
            s = jnp.where(seq_ref[0] >= hop, s, MASKED)
        scores.append(s)
    peak = functools.reduce(jnp.maximum, [jnp.max(s, axis=1, keepdims=True) for s in scores])
    weights = [jnp.exp(s - peak) for s in scores]
    total = functools.reduce(jnp.add, [jnp.sum(w, axis=1, keepdims=True) for w in weights])
    scale = 1.0 / total
    out = None
    for hop in range(hops + 1):
        part = dot((weights[hop] * scale).astype(BF16), values[hop][0])
        out = part if out is None else out + part
    if len(refs) == 2 * hops + 3:
        out_ref[...] = out
    else:
        fast_ref, gain_ref, inv_ref = refs[2 * hops + 2 : 2 * hops + 5]
        out_ref[0] = (fast_ref[...] * gain_ref[...] * inv_ref[...] + out).astype(BF16)


def attend(seq, stretch, queries, keys, values, heads, normed=None):
    stretches, tok, feat = queries.shape
    size = feat // heads
    hops = len(keys) - 1

    def rows_of(hop):
        def index(h, seq_ref):
            back = jnp.where(seq_ref[0] < hop, 1, 0)
            return (jnp.maximum(stretch - back, 0), 0, h)

        return pl.BlockSpec((1, tok, size), index)

    token_specs = [rows_of(hop) for hop in range(hops + 1)]
    in_specs = [pl.BlockSpec((1, tok, size), lambda h, s: (stretch, 0, h))] + token_specs * 2
    operands = [seq, queries, *keys, *values]
    if normed is None:
        out_specs = pl.BlockSpec((tok, size), lambda h, s: (0, h))
        out_shape = jax.ShapeDtypeStruct((tok, feat), F32)
    else:
        operands += list(normed)
        in_specs += [
            pl.BlockSpec((tok, size), lambda h, s: (0, h)),
            pl.BlockSpec((1, size), lambda h, s: (0, h)),
            pl.BlockSpec((tok, 1), lambda h, s: (0, 0)),
        ]
        out_specs = pl.BlockSpec((1, tok, size), lambda h, s: (stretch, 0, h))
        out_shape = jax.ShapeDtypeStruct((stretches, tok, feat), BF16)
    return pl.pallas_call(
        functools.partial(attend_kernel, hops, stretch),
        grid_spec=pltpu.PrefetchScalarGridSpec(
            num_scalar_prefetch=1,
            grid=(heads,),
            in_specs=in_specs,
            out_specs=out_specs,
        ),
        out_shape=out_shape,
        compiler_params=params(),
        cost_estimate=pl.CostEstimate(
            flops=feat * tok * tok * (hops + 1) * 4 * 2,
            bytes_accessed=feat * tok * (2 * (2 * hops + 3) + 4),
            transcendentals=heads * tok * tok * (hops + 1),
        ),
        name="attend",
    )(*operands)


def final_kernel(stretch, base_ref, fast_ref, gain_ref, inv_ref, att_ref, out_ref):
    out_ref[0] = (fast_ref[...] * gain_ref[...] * inv_ref[...] + att_ref[...]).astype(BF16)


def finish(base, stretch, fast, gain, inv, att, parts):
    _, tok, feat = base.shape
    size = feat // parts
    tall = pl.BlockSpec((tok, size), lambda h: (0, h))
    return pl.pallas_call(
        functools.partial(final_kernel, stretch),
        grid=(parts,),
        in_specs=[
            pl.BlockSpec(memory_space=pl.ANY),
            tall,
            pl.BlockSpec((1, size), lambda h: (0, h)),
            pl.BlockSpec((tok, 1), lambda h: (0, 0)),
            tall,
        ],
        out_specs=pl.BlockSpec((1, tok, size), lambda h: (stretch, 0, h)),
        out_shape=jax.ShapeDtypeStruct(base.shape, base.dtype),
        input_output_aliases={0: 0},
        compiler_params=params(),
        name="finish",
    )(base, fast, gain, inv, att)


def on_device(queries, key_rows, value_rows, step_rates, w_gate, w_up, w_down, out_gain):
    stretches, tok, feat = queries.shape
    heads = w_gate.shape[0]
    seq = lax.axis_index("seq").astype(jnp.int32).reshape(1)
    hops = -(-WINDOW // tok)
    features = feat * lax.axis_size("heads")
    gain = out_gain.reshape(1, feat)

    def inverse_norm(power):
        total = lax.psum(power.reshape(tok), "heads")
        return lax.rsqrt(total / features + NORM_EPS).reshape(tok, 1)

    masters = jnp.stack([w_gate, w_up, w_down], axis=1)
    copies = gather_two_level(masters.astype(BF16))
    keys, values = [key_rows], [value_rows]
    keys.append(passed_along(key_rows, "seq", 1))
    values.append(passed_along(value_rows, "seq", 1))
    copies, keys[1], values[1] = lax.optimization_barrier((copies, keys[1], values[1]))
    for _ in range(1, hops):
        keys.append(passed_along(keys[-1], "seq", 1))
        values.append(passed_along(values[-1], "seq", 1))

    gradients = fast_grads(copies, key_rows, value_rows, step_rates[:, 0, :].T)
    total = scatter_two_level(gradients)
    fast_0, power_0 = fast_apply(copies, queries, 0)
    inv_0 = inverse_norm(power_0)
    total, keys, values, fast_0, inv_0 = lax.optimization_barrier(
        (total, keys, values, fast_0, inv_0)
    )
    updated = masters - total.astype(F32)
    second = gather_two_level(updated.astype(BF16))
    layer_0 = attend(seq, 0, queries, keys, values, heads, (fast_0, gain, inv_0))
    attended_1 = attend(seq, 1, queries, keys, values, heads)
    second, layer_0, attended_1 = lax.optimization_barrier((second, layer_0, attended_1))
    fast_1, power_1 = fast_apply(second, queries, 1)
    layer_out = finish(layer_0, 1, fast_1, gain, inverse_norm(power_1), attended_1, heads)
    return (layer_out, updated[:, 0], updated[:, 1], updated[:, 2])


def solution(mesh):
    rows = P(None, "seq", "heads")
    weights = P("heads", "seq", None)
    return jax.shard_map(
        on_device,
        mesh=mesh,
        in_specs=(rows, rows, rows, P("heads", None, "seq"), weights, weights, weights, P("heads")),
        out_specs=(rows, weights, weights, weights),
        check_vma=False,
    )
```
